128 devices in a mesh: cp: 64 (over x, y, z), hd: 2 (over core).
Axes of the slice: x: 4, y: 4, z: 4, core: 2. Of those that a mesh axis runs over, the one named last changes fastest.
Arguments:
- doc_lengths: int32 [16], replicated, may hold values from 1 to 1792, 16384 in all
- queries: bfloat16 [16384, 4096], P(('cp', 'hd')), may hold values from -6 to 6, as said below
- keys: bfloat16 [16384, 1024], P(('cp', 'hd')), may hold values from -6 to 6, as said below
- values: bfloat16 [16384, 1024], P(('cp', 'hd')), may hold values from -6 to 6
- output_gradient: bfloat16 [16384, 4096], P(('cp', 'hd')), may hold values from -6 to 6
Outputs:
- attended: bfloat16 [16384, 4096], P(('cp', 'hd'))
- grad_queries: bfloat16 [16384, 4096], P(('cp', 'hd'))
- grad_keys: bfloat16 [16384, 1024], P(('cp', 'hd'))
- grad_values: bfloat16 [16384, 1024], P(('cp', 'hd'))
The draws below stay inside these ranges and needn't reach their ends.
Inputs may be any that keep to these rules, and one draw needn't show every extreme that they name: `doc_lengths`: documents lie end to end and sum to 16384 tokens; the longest has exactly 1792. `queries`: entries of order one. `keys`: entries of order one.
All inputs are finite; a program needn't handle non-finite values.
Results may differ from the reference program's by a relative error of at most 0.012.
The reference program's roundings to bfloat16 on the way count: a program that leaves them out, or rounds other values in their place, can miss the bound.
Values may be sent and summed in bfloat16 or wider, within the bound.
No kernel may reach another device: no remote copies, remote signals or barrier semaphores. Data moves between devices by JAX's collectives and lax.ppermute only.
A program may use at most 128 MiB of HBM per device.

```python
import math
import jax
import jax.numpy as jnp
import numpy as np
from jax import lax

QUERY_HEAD_COUNT = 32
KEY_VALUE_HEADS = 8
HEAD_SIZE = 128
TOK_DEV = 256
SPAN = 7
PACK_TOKENS = 16384
MOST = 1792
DOCS = 16
N_CP = 64


def draw_queries(key, part):
    key = jax.random.fold_in(key, 1)
    base_offset = jnp.clip(jax.random.normal(key, (PACK_TOKENS, QUERY_HEAD_COUNT * HEAD_SIZE), jnp.float32), -6.0, 6.0)
    return base_offset.astype(jnp.bfloat16)


def draw_keys(key, part):
    key = jax.random.fold_in(key, 2)
    base_offset = jnp.clip(jax.random.normal(key, (PACK_TOKENS, KEY_VALUE_HEADS * HEAD_SIZE), jnp.float32), -6.0, 6.0)
    return base_offset.astype(jnp.bfloat16)


def level_of(key, extent, cuts, least, top_value):
    loudness, own = 1.0, jax.random.fold_in(key, 6)
    for position, blocks in cuts:
        heights = jnp.exp(jax.random.uniform(jax.random.fold_in(own, position), (blocks,), jnp.float32, least / len(cuts), top_value / len(cuts)))
        loudness = loudness * jnp.repeat(heights, extent[position] // blocks).reshape([-1 if axis == position else 1 for axis in range(len(extent))])
    return loudness


def profile(amount, total, limit, lean):
    portions = [(1 << 20) // math.isqrt(rank ** lean) + 1 for rank in range(2, amount + 1)]
    rest, holding = total - limit - (amount - 1), [1] * (amount - 1)
    while rest > 0:
        free = [i for i in range(amount - 1) if holding[i] < limit]
        mass, left = sum([portions[i] for i in free]), rest
        for i in free:
            addition = min(limit - holding[i], max(1, left * portions[i] // mass), rest)
            holding[i] = holding[i] + addition
            rest = rest - addition
    return np.array([limit] + holding)


def uneven_parts(key, amount, total, most, slope):
    if amount == 2:
        one = jax.random.randint(key, (), max(1, total - most), min(most, total - 1) + 1)
        return jnp.stack([one, total - one])
    tallies = jnp.asarray(profile(amount, total, most, slope), jnp.int32)
    couples = (amount - 1) // 2
    giver, receiver = tallies[1:1 + 2 * couples:2], tallies[2:2 + 2 * couples:2]
    margin = jnp.minimum(giver - 1, most - receiver)
    moved = jax.random.randint(jax.random.fold_in(key, 1), (couples,), 0, 1 << 20) % (margin + 1)
    tallies = tallies.at[1:1 + 2 * couples:2].set(giver - moved).at[2:2 + 2 * couples:2].set(receiver + moved)
    return tallies[jax.random.permutation(jax.random.fold_in(key, 2), amount)]


def bell_draw(own_key, shape, spread, limit, split=(), kind=jnp.bfloat16):
    result = spread * jax.random.normal(own_key, shape, jnp.float32)
    if split:
        result = result * level_of(own_key, shape, split, -0.22, 0.18)
    return jnp.clip(result, -limit, limit).astype(kind)


def setup_inputs(seed: int = 0) -> dict:
    streams_of = jax.random.split(jax.random.key(seed), 6)
    return {
        "doc_lengths": uneven_parts(streams_of[0], DOCS, PACK_TOKENS, MOST, 2).astype(jnp.int32),
        "queries": draw_queries(jax.random.fold_in(streams_of[5], 71), 0),
        "keys": draw_keys(jax.random.fold_in(streams_of[5], 71), 0),
        "values": bell_draw(streams_of[3], (PACK_TOKENS, KEY_VALUE_HEADS * HEAD_SIZE), 1.0, 6.0, ((0, 128),)),
        "output_gradient": bell_draw(streams_of[4], (PACK_TOKENS, QUERY_HEAD_COUNT * HEAD_SIZE), 1.0, 6.0, ((0, 128),)),
    }


def segment_ids(doc_lengths, positions):
    ends = jnp.cumsum(doc_lengths).astype(jnp.int32)
    return jnp.sum((positions[:, None] >= ends[None, :]).astype(jnp.int32), axis=1).astype(jnp.int32)


def reference(doc_lengths, queries, keys, values, output_gradient):
    block_span = TOK_DEV
    key_window = (SPAN + 1) * block_span
    head_group = QUERY_HEAD_COUNT // KEY_VALUE_HEADS
    scale = HEAD_SIZE ** -0.5
    leading_offset = SPAN * block_span
    segment = segment_ids(doc_lengths, jnp.arange(PACK_TOKENS, dtype=jnp.int32))
    seg_padded = jnp.concatenate([-jnp.ones((leading_offset,), jnp.int32), segment])
    padded_keys = jnp.concatenate([jnp.zeros((leading_offset, KEY_VALUE_HEADS * HEAD_SIZE), jnp.bfloat16), keys])
    padded_values = jnp.concatenate([jnp.zeros((leading_offset, KEY_VALUE_HEADS * HEAD_SIZE), jnp.bfloat16), values])
    running_totals = jnp.zeros((2, PACK_TOKENS + leading_offset, KEY_VALUE_HEADS * HEAD_SIZE), jnp.float32)

    def step(carry, index):
        start_index = (index * block_span).astype(jnp.int32)
        query_block_rows = lax.dynamic_slice_in_dim(queries, start_index, block_span, 0).astype(jnp.float32).reshape(block_span, KEY_VALUE_HEADS, head_group, HEAD_SIZE)
        gradient_rows = lax.dynamic_slice_in_dim(output_gradient, start_index, block_span, 0).astype(jnp.float32).reshape(block_span, KEY_VALUE_HEADS, head_group, HEAD_SIZE)
        key_block_rows = lax.dynamic_slice_in_dim(padded_keys, start_index, key_window, 0).astype(jnp.float32).reshape(key_window, KEY_VALUE_HEADS, HEAD_SIZE)
        value_block_rows = lax.dynamic_slice_in_dim(padded_values, start_index, key_window, 0).astype(jnp.float32).reshape(key_window, KEY_VALUE_HEADS, HEAD_SIZE)
        seg_query = lax.dynamic_slice_in_dim(segment, start_index, block_span, 0)
        seg_key = lax.dynamic_slice_in_dim(seg_padded, start_index, key_window, 0)
        query_pos = start_index + jnp.arange(block_span, dtype=jnp.int32)
        key_pos = start_index - leading_offset + jnp.arange(key_window, dtype=jnp.int32)
        allowed = (key_pos[None, :] >= 0) & (seg_key[None, :] == seg_query[:, None]) & (key_pos[None, :] <= query_pos[:, None])
        scores = jnp.einsum("bhgd,whd->hgbw", query_block_rows, key_block_rows) * scale
        scores = jnp.where(allowed[None, None], scores, -jnp.inf)
        peak = jnp.max(scores, axis=-1, keepdims=True)
        expo = jnp.exp(scores - peak)
        probs = expo / jnp.sum(expo, axis=-1, keepdims=True)
        narrow_probabilities = lax.optimization_barrier(probs.astype(jnp.bfloat16)).astype(jnp.float32)
        attended = jnp.einsum("hgbw,whd->bhgd", narrow_probabilities, value_block_rows).astype(jnp.bfloat16)
        attended_wide = lax.optimization_barrier(attended).astype(jnp.float32)
        dprobs = jnp.einsum("bhgd,whd->hgbw", gradient_rows, value_block_rows)
        delta = jnp.einsum("bhgd,bhgd->hgb", gradient_rows, attended_wide)
        score_gradient = (probs * (dprobs - delta[..., None]) * scale).astype(jnp.bfloat16)
        score_gradient = lax.optimization_barrier(score_gradient).astype(jnp.float32)
        grad_q = jnp.einsum("hgbw,whd->bhgd", score_gradient, key_block_rows).astype(jnp.bfloat16)
        key_gradient = jnp.einsum("vpnm,nvpc->mvc", score_gradient, query_block_rows).reshape(key_window, KEY_VALUE_HEADS * HEAD_SIZE)
        value_gradient = jnp.einsum("vpnm,nvpc->mvc", narrow_probabilities, gradient_rows).reshape(key_window, KEY_VALUE_HEADS * HEAD_SIZE)
        current = lax.dynamic_slice_in_dim(carry, start_index, key_window, 1)
        carry = lax.dynamic_update_slice_in_dim(carry, current + jnp.stack([key_gradient, value_gradient]), start_index, 1)
        return carry, (attended.reshape(block_span, QUERY_HEAD_COUNT * HEAD_SIZE), grad_q.reshape(block_span, QUERY_HEAD_COUNT * HEAD_SIZE))

    running_totals, (attended_all, grad_q_all) = lax.scan(step, running_totals, jnp.arange(N_CP, dtype=jnp.int32))
    grad_keys = running_totals[0, leading_offset:].astype(jnp.bfloat16)
    grad_values = running_totals[1, leading_offset:].astype(jnp.bfloat16)
    return attended_all.reshape(PACK_TOKENS, QUERY_HEAD_COUNT * HEAD_SIZE), grad_q_all.reshape(PACK_TOKENS, QUERY_HEAD_COUNT * HEAD_SIZE), grad_keys, grad_values
```

```python
import jax
import jax.numpy as jnp
from jax import lax
from jax.experimental import pallas as pl
from jax.experimental.pallas import tpu as pltpu
from jax.sharding import Mesh, PartitionSpec as P

HEAD = 128
GROUP = 4
BLOCK = 256
ROW = 1024
BEHIND = 1792
WINDOW = BEHIND + ROW
TILES = ROW // BLOCK
REACH = BEHIND // BLOCK + 1
WIDE = GROUP * BLOCK
SCALE = HEAD ** (-0.5)
LOG2E = 1.4426950408889634
AXES = ("x", "y", "z", "hd")
ROWS = ("z", "hd")

NT = (((1,), (1,)), ((), ()))
TN = (((0,), (0,)), ((), ()))
NN = (((1,), (0,)), ((), ()))


def dot(a, b, dims):
    return lax.dot_general(a, b, dims, preferred_element_type=jnp.float32)


def attention_kernel(
    doc_ref, qg_ref, kv2_ref, kv1_ref, kv0_ref, out_ref, d2_ref, d1_ref, d0_ref, kv, acc, scores, oacc, qacc
):
    tile = pl.program_id(0)
    row = lax.axis_index("x") * 4 + lax.axis_index("y")

    @pl.when(tile == 0)
    def _():
        kv[0:768] = kv2_ref[...]
        kv[768:1792] = kv1_ref[...]
        kv[1792:2816] = kv0_ref[...]
        acc[...] = jnp.zeros_like(acc)

    origin = row * ROW - BEHIND
    first_query = BEHIND + tile * BLOCK
    query_at = first_query + lax.broadcasted_iota(jnp.int32, (1, BLOCK), 1)
    start_at = jnp.full((1, BLOCK), -origin, jnp.int32)
    first_start = -origin
    end = -origin
    for n in range(16):
        end = end + doc_ref[n]
        start_at = jnp.where(query_at >= end, end, start_at)
        first_start = jnp.where(first_query >= end, end, first_start)
    low = first_start // BLOCK
    high = REACH + tile

    qg = qg_ref[...].reshape(BLOCK, 2 * GROUP * HEAD)
    q = jnp.concatenate([qg[:, h * HEAD : (h + 1) * HEAD] for h in range(GROUP)], axis=0)
    g = jnp.concatenate([qg[:, (GROUP + h) * HEAD : (GROUP + h + 1) * HEAD] for h in range(GROUP)], axis=0)

    def score_step(j, peak):
        at = pl.multiple_of(j * BLOCK, BLOCK)
        k = kv[pl.ds(at, BLOCK), :HEAD]
        s = dot(k, q, NT)
        key_at = at + lax.broadcasted_iota(jnp.int32, (BLOCK, BLOCK), 0)
        allowed = (key_at >= start_at) & (key_at <= query_at)
        s = jnp.where(jnp.concatenate([allowed] * GROUP, axis=1), s, -jnp.inf)
        scores[j - tile] = s
        return jnp.maximum(peak, jnp.max(s.reshape(BLOCK // 8, 8, WIDE), axis=0))

    peak = lax.fori_loop(low, high, score_step, jnp.full((8, WIDE), -jnp.inf, jnp.float32))
    peak = jnp.max(peak, axis=0, keepdims=True)

    def exp_step(j, total):
        e = jnp.exp2((scores[j - tile] - peak) * (SCALE * LOG2E))
        scores[j - tile] = e
        return total + jnp.sum(e.reshape(BLOCK // 8, 8, WIDE), axis=0)

    total = lax.fori_loop(low, high, exp_step, jnp.zeros((8, WIDE), jnp.float32))
    inverse = 1.0 / jnp.sum(total, axis=0, keepdims=True)

    oacc[...] = jnp.zeros_like(oacc)
    qacc[...] = jnp.zeros_like(qacc)

    def out_step(j, _):
        at = pl.multiple_of(j * BLOCK, BLOCK)
        v = kv[pl.ds(at, BLOCK), HEAD:]
        p = (scores[j - tile] * inverse).astype(jnp.bfloat16)
        oacc[...] += dot(p, v, TN)
        acc[pl.ds(at, BLOCK), HEAD:] += dot(p, g, NN)
        return 0

    lax.fori_loop(low, high, out_step, 0)
    attended = oacc[...].astype(jnp.bfloat16)
    delta = attended.astype(jnp.float32) * g.astype(jnp.float32)
    delta = jnp.sum(delta.T, axis=0, keepdims=True)
    inverse = inverse * SCALE

    def grad_step(j, _):
        at = pl.multiple_of(j * BLOCK, BLOCK)
        k = kv[pl.ds(at, BLOCK), :HEAD]
        v = kv[pl.ds(at, BLOCK), HEAD:]
        dp = dot(v, g, NT)
        ds = (scores[j - tile] * inverse * (dp - delta)).astype(jnp.bfloat16)
        qacc[...] += dot(ds, k, TN)
        acc[pl.ds(at, BLOCK), :HEAD] += dot(ds, q, NN)
        return 0

    lax.fori_loop(low, high, grad_step, 0)
    grad_q = qacc[...].astype(jnp.bfloat16)
    for h in range(GROUP):
        for half in range(2):
            rows = slice(h * BLOCK + half * 128, h * BLOCK + half * 128 + 128)
            out_ref[half, :, h * HEAD : (h + 1) * HEAD] = attended[rows]
            out_ref[half, :, (GROUP + h) * HEAD : (GROUP + h + 1) * HEAD] = grad_q[rows]

    @pl.when(tile == TILES - 1)
    def _():
        d2_ref[...] = acc[0:768].astype(jnp.bfloat16)
        d1_ref[...] = acc[768:1792].astype(jnp.bfloat16)
        d0_ref[...] = acc[1792:2816]


def attention(doc_lengths, qg, kv2, kv1, kv0):
    whole = lambda *shape: pl.BlockSpec(shape, lambda i: (0,) * len(shape))
    tiled = pl.BlockSpec((2, 128, 2 * GROUP * HEAD), lambda i: (i, 0, 0))
    return pl.pallas_call(
        attention_kernel,
        grid=(TILES,),
        in_specs=[
            pl.BlockSpec(memory_space=pltpu.SMEM),
            tiled,
            whole(768, 256),
            whole(1024, 256),
            whole(1024, 256),
        ],
        out_specs=[tiled, whole(768, 256), whole(1024, 256), whole(1024, 256)],
        out_shape=[
            jax.ShapeDtypeStruct((8, 128, 2 * GROUP * HEAD), jnp.bfloat16),
            jax.ShapeDtypeStruct((768, 256), jnp.bfloat16),
            jax.ShapeDtypeStruct((1024, 256), jnp.bfloat16),
            jax.ShapeDtypeStruct((1024, 256), jnp.float32),
        ],
        scratch_shapes=[
            pltpu.VMEM((WINDOW, 256), jnp.bfloat16),
            pltpu.VMEM((WINDOW, 256), jnp.float32),
            pltpu.VMEM((REACH, BLOCK, WIDE), jnp.float32),
            pltpu.VMEM((WIDE, HEAD), jnp.float32),
            pltpu.VMEM((WIDE, HEAD), jnp.float32),
        ],
        compiler_params=pltpu.CompilerParams(vmem_limit_bytes=48 * 1024 * 1024),
        name="attention",
    )(doc_lengths, qg, kv2, kv1, kv0)


def shift(x, by):
    pairs = [(i, i + by) for i in range(64) if 0 <= i + by < 64]
    return lax.ppermute(x, ("x", "y", "z"), pairs)


def swap(x):
    return lax.all_to_all(x, ROWS, split_axis=0, concat_axis=0, tiled=False)


def pack(a, b):
    tokens = a.shape[0]
    both = jnp.concatenate([a.reshape(tokens, 8, -1), b.reshape(tokens, 8, -1)], axis=2)
    return both.transpose(1, 0, 2)


def unpack(x):
    half = x.shape[2] // 2
    return [
        part.transpose(1, 0, 2).reshape(x.shape[1], 8 * half) for part in (x[:, :, :half], x[:, :, half:])
    ]


def body(doc_lengths, queries, keys, values, output_gradient):
    kv0 = swap(pack(keys, values)).reshape(ROW, 256)
    kv1 = shift(kv0, 4)
    kv2 = shift(kv0[256:], 8)
    qg = swap(pack(queries, output_gradient))
    out, d2, d1, d0 = attention(doc_lengths, qg, kv2, kv1, kv0)
    d1 = shift(d1, -4).astype(jnp.float32)
    d2 = shift(d2, -8).astype(jnp.float32)
    total = d0 + d1 + jnp.pad(d2, ((256, 0), (0, 0)))
    grad_keys, grad_values = unpack(swap(total.astype(jnp.bfloat16).reshape(8, 128, 256)))
    attended, grad_queries = unpack(swap(out))
    return attended, grad_queries, grad_keys, grad_values


def solution(mesh):
    grid = Mesh(mesh.devices.reshape(4, 4, 4, 2), AXES)
    tokens = P(AXES, None)
    return jax.shard_map(
        body,
        mesh=grid,
        in_specs=(P(None), tokens, tokens, tokens, tokens),
        out_specs=(tokens, tokens, tokens, tokens),
        check_vma=False,
    )
```

```python
import jax
import jax.numpy as jnp
from jax import lax
from jax.experimental import pallas as pl
from jax.experimental.pallas import tpu as pltpu
from jax.sharding import Mesh, PartitionSpec as P

HEAD = 128
GROUP = 4
BLOCK = 256
ROW = 1024
BEHIND = 1792
WINDOW = BEHIND + ROW
TILES = ROW // BLOCK
REACH = BEHIND // BLOCK + 1
WIDE = GROUP * BLOCK
SCALE = HEAD ** (-0.5)
LOG2E = 1.4426950408889634
AXES = ("x", "y", "z", "hd")
ROWS = ("z", "hd")

NT = (((1,), (1,)), ((), ()))
TN = (((0,), (0,)), ((), ()))
NN = (((1,), (0,)), ((), ()))


def dot(a, b, dims):
    return lax.dot_general(a, b, dims, preferred_element_type=jnp.float32)


def attention_kernel(
    doc_ref, qg_ref, kv2_ref, kv1_ref, kv0_ref, out_ref, d2_ref, d1_ref, d0_ref, kv, acc, scores, oacc, qacc
):
    tile = pl.program_id(0)
    row = lax.axis_index("x") * 4 + lax.axis_index("y")

    @pl.when(tile == 0)
    def _():
        kv[0:768] = kv2_ref[...]
        kv[768:1792] = kv1_ref[...]
        kv[1792:2816] = kv0_ref[...]
        acc[...] = jnp.zeros_like(acc)

    origin = row * ROW - BEHIND
    first_query = BEHIND + tile * BLOCK
    query_at = first_query + lax.broadcasted_iota(jnp.int32, (1, BLOCK), 1)
    start_at = jnp.full((1, BLOCK), -origin, jnp.int32)
    first_start = -origin
    end = -origin
    for n in range(16):
        end = end + doc_ref[n]
        start_at = jnp.where(query_at >= end, end, start_at)
        first_start = jnp.where(first_query >= end, end, first_start)
    low = first_start // BLOCK
    high = REACH + tile

    qg = qg_ref[...].reshape(BLOCK, 2 * GROUP * HEAD)
    q = jnp.concatenate([qg[:, h * HEAD : (h + 1) * HEAD] for h in range(GROUP)], axis=0)
    g = jnp.concatenate([qg[:, (GROUP + h) * HEAD : (GROUP + h + 1) * HEAD] for h in range(GROUP)], axis=0)

    def score_step(j, peak):
        at = pl.multiple_of(j * BLOCK, BLOCK)
        k = kv[pl.ds(at, BLOCK), :HEAD]
        s = dot(k, q, NT)
        key_at = at + lax.broadcasted_iota(jnp.int32, (BLOCK, BLOCK), 0)
        allowed = (key_at >= start_at) & (key_at <= query_at)
        s = jnp.where(jnp.concatenate([allowed] * GROUP, axis=1), s, -jnp.inf)
        scores[j - tile] = s
        return jnp.maximum(peak, jnp.max(s.reshape(BLOCK // 8, 8, WIDE), axis=0))

    peak = lax.fori_loop(low, high, score_step, jnp.full((8, WIDE), -jnp.inf, jnp.float32))
    peak = jnp.max(peak, axis=0, keepdims=True)

    def exp_step(j, total):
        e = jnp.exp2((scores[j - tile] - peak) * (SCALE * LOG2E))
        scores[j - tile] = e
        return total + jnp.sum(e.reshape(BLOCK // 8, 8, WIDE), axis=0)

    total = lax.fori_loop(low, high, exp_step, jnp.zeros((8, WIDE), jnp.float32))
    inverse = 1.0 / jnp.sum(total, axis=0, keepdims=True)

    oacc[...] = jnp.zeros_like(oacc)
    qacc[...] = jnp.zeros_like(qacc)

    def out_step(j, _):
        at = pl.multiple_of(j * BLOCK, BLOCK)
        v = kv[pl.ds(at, BLOCK), HEAD:]
        p = (scores[j - tile] * inverse).astype(jnp.bfloat16)
        oacc[...] += dot(p, v, TN)
        acc[pl.ds(at, BLOCK), HEAD:] += dot(p, g, NN)
        return 0

    lax.fori_loop(low, high, out_step, 0)
    attended = oacc[...].astype(jnp.bfloat16)
    delta = attended.astype(jnp.float32) * g.astype(jnp.float32)
    delta = jnp.sum(delta.T, axis=0, keepdims=True)
    inverse = inverse * SCALE

    def grad_step(j, _):
        at = pl.multiple_of(j * BLOCK, BLOCK)
        k = kv[pl.ds(at, BLOCK), :HEAD]
        v = kv[pl.ds(at, BLOCK), HEAD:]
        dp = dot(v, g, NT)
        ds = (scores[j - tile] * inverse * (dp - delta)).astype(jnp.bfloat16)
        qacc[...] += dot(ds, k, TN)
        acc[pl.ds(at, BLOCK), :HEAD] += dot(ds, q, NN)
        return 0

    lax.fori_loop(low, high, grad_step, 0)
    grad_q = qacc[...].astype(jnp.bfloat16)
    for h in range(GROUP):
        for half in range(2):
            rows = slice(h * BLOCK + half * 128, h * BLOCK + half * 128 + 128)
            out_ref[half, :, h * HEAD : (h + 1) * HEAD] = attended[rows]
            out_ref[half, :, (GROUP + h) * HEAD : (GROUP + h + 1) * HEAD] = grad_q[rows]

    @pl.when(tile == TILES - 1)
    def _():
        d2_ref[...] = acc[0:768].astype(jnp.bfloat16)
        d1_ref[...] = acc[768:1792].astype(jnp.bfloat16)
        d0_ref[...] = acc[1792:2816]


def attention(doc_lengths, qg, kv2, kv1, kv0):
    whole = lambda *shape: pl.BlockSpec(shape, lambda i: (0,) * len(shape))
    tiled = pl.BlockSpec((2, 128, 2 * GROUP * HEAD), lambda i: (i, 0, 0))
    return pl.pallas_call(
        attention_kernel,
        grid=(TILES,),
        in_specs=[
            pl.BlockSpec(memory_space=pltpu.SMEM),
            tiled,
            whole(768, 256),
            whole(1024, 256),
            whole(1024, 256),
        ],
        out_specs=[tiled, whole(768, 256), whole(1024, 256), whole(1024, 256)],
        out_shape=[
            jax.ShapeDtypeStruct((8, 128, 2 * GROUP * HEAD), jnp.bfloat16),
            jax.ShapeDtypeStruct((768, 256), jnp.bfloat16),
            jax.ShapeDtypeStruct((1024, 256), jnp.bfloat16),
            jax.ShapeDtypeStruct((1024, 256), jnp.float32),
        ],
        scratch_shapes=[
            pltpu.VMEM((WINDOW, 256), jnp.bfloat16),
            pltpu.VMEM((WINDOW, 256), jnp.float32),
            pltpu.VMEM((REACH, BLOCK, WIDE), jnp.float32),
            pltpu.VMEM((WIDE, HEAD), jnp.float32),
            pltpu.VMEM((WIDE, HEAD), jnp.float32),
        ],
        compiler_params=pltpu.CompilerParams(vmem_limit_bytes=48 * 1024 * 1024),
        name="attention",
    )(doc_lengths, qg, kv2, kv1, kv0)


def shift(x, by):
    pairs = [(i, i + by) for i in range(64) if 0 <= i + by < 64]
    return lax.ppermute(x, ("x", "y", "z"), pairs)


def swap(x):
    return lax.all_to_all(x, ROWS, split_axis=0, concat_axis=0, tiled=False)


def pack(a, b):
    tokens = a.shape[0]
    both = jnp.concatenate([a.reshape(tokens, 8, -1), b.reshape(tokens, 8, -1)], axis=2)
    return both.transpose(1, 0, 2)


def unpack(x):
    half = x.shape[2] // 2
    return [
        part.transpose(1, 0, 2).reshape(x.shape[1], 8 * half) for part in (x[:, :, :half], x[:, :, half:])
    ]


def body(doc_lengths, queries, keys, values, output_gradient):
    kv0 = swap(pack(keys, values)).reshape(ROW, 256)
    kv1 = shift(kv0, 4)
    kv2 = shift(kv0[256:], 8)
    qg = swap(pack(queries, output_gradient))
    out, d2, d1, d0 = attention(doc_lengths, qg, kv2, kv1, kv0)
    d1 = shift(d1, -4).astype(jnp.float32)
    d2 = shift(d2, -8).astype(jnp.float32)
    total = d0 + d1 + jnp.pad(d2, ((256, 0), (0, 0)))
    total, out = lax.optimization_barrier((total.astype(jnp.bfloat16), swap(out)))
    grad_keys, grad_values = unpack(swap(total.reshape(8, 128, 256)))
    attended, grad_queries = unpack(out)
    return attended, grad_queries, grad_keys, grad_values


def solution(mesh):
    grid = Mesh(mesh.devices.reshape(4, 4, 4, 2), AXES)
    tokens = P(AXES, None)
    return jax.shard_map(
        body,
        mesh=grid,
        in_specs=(P(None), tokens, tokens, tokens, tokens),
        out_specs=(tokens, tokens, tokens, tokens),
        check_vma=False,
    )
```

```python
import jax
import jax.numpy as jnp
from jax import lax
from jax.experimental import pallas as pl
from jax.experimental.pallas import tpu as pltpu
from jax.sharding import Mesh, PartitionSpec as P

HEAD = 128
GROUP = 4
BLOCK = 256
STEP = 512
ROW = 1024
BEHIND = 1792
WINDOW = BEHIND + ROW
TILES = ROW // BLOCK
SLOTS = (BEHIND + 2 * BLOCK) // STEP + 1
WIDE = GROUP * BLOCK
SCALE = HEAD ** (-0.5)
LOG2E = 1.4426950408889634
AXES = ("x", "y", "z", "hd")
ROWS = ("z", "hd")

NT = (((1,), (1,)), ((), ()))
TN = (((0,), (0,)), ((), ()))
NN = (((1,), (0,)), ((), ()))


def dot(a, b, dims):
    return lax.dot_general(a, b, dims, preferred_element_type=jnp.float32)


def attention_kernel(
    doc_ref, qg_ref, kv2_ref, kv1_ref, kv0_ref, out_ref, d2_ref, d1_ref, d0_ref, kv, acc, scores, oacc, qacc
):
    tile = pl.program_id(0)
    row = lax.axis_index("x") * 4 + lax.axis_index("y")

    @pl.when(tile == 0)
    def _():
        kv[0:768] = kv2_ref[...]
        kv[768:1792] = kv1_ref[...]
        kv[1792:2816] = kv0_ref[...]
        kv[2816:] = jnp.zeros((STEP, 256), jnp.bfloat16)
        acc[...] = jnp.zeros_like(acc)

    origin = row * ROW - BEHIND
    first_query = BEHIND + tile * BLOCK
    query_at = first_query + lax.broadcasted_iota(jnp.int32, (1, BLOCK), 1)
    start_at = jnp.full((1, BLOCK), -origin, jnp.int32)
    first_start = -origin
    end = -origin
    for n in range(16):
        end = end + doc_ref[n]
        start_at = jnp.where(query_at >= end, end, start_at)
        first_start = jnp.where(first_query >= end, end, first_start)
    low = first_start // BLOCK * BLOCK
    count = (first_query + BLOCK - low + STEP - 1) // STEP

    qg = qg_ref[...].reshape(BLOCK, 2 * GROUP * HEAD)
    q = jnp.concatenate([qg[:, h * HEAD : (h + 1) * HEAD] for h in range(GROUP)], axis=0)
    g = jnp.concatenate([qg[:, (GROUP + h) * HEAD : (GROUP + h + 1) * HEAD] for h in range(GROUP)], axis=0)

    def score_step(n, peak):
        at = pl.multiple_of(low + n * STEP, BLOCK)
        k = kv[pl.ds(at, STEP), :HEAD]
        s = dot(k, q, NT)
        key_at = at + lax.broadcasted_iota(jnp.int32, (STEP, BLOCK), 0)
        allowed = (key_at >= start_at) & (key_at <= query_at)
        s = jnp.where(jnp.concatenate([allowed] * GROUP, axis=1), s, -jnp.inf)
        scores[n] = s
        return jnp.maximum(peak, jnp.max(s.reshape(STEP // 8, 8, WIDE), axis=0))

    peak = lax.fori_loop(0, count, score_step, jnp.full((8, WIDE), -jnp.inf, jnp.float32))
    peak = jnp.max(peak, axis=0, keepdims=True)

    def exp_step(n, total):
        e = jnp.exp2((scores[n] - peak) * (SCALE * LOG2E))
        scores[n] = e
        return total + jnp.sum(e.reshape(STEP // 8, 8, WIDE), axis=0)

    total = lax.fori_loop(0, count, exp_step, jnp.zeros((8, WIDE), jnp.float32))
    inverse = 1.0 / jnp.sum(total, axis=0, keepdims=True)

    oacc[...] = jnp.zeros_like(oacc)
    qacc[...] = jnp.zeros_like(qacc)

    def out_step(n, _):
        at = pl.multiple_of(low + n * STEP, BLOCK)
        v = kv[pl.ds(at, STEP), HEAD:]
        p = (scores[n] * inverse).astype(jnp.bfloat16)
        oacc[...] += dot(v, p, TN)
        acc[pl.ds(at, STEP), HEAD:] += dot(p, g, NN)
        return 0

    lax.fori_loop(0, count, out_step, 0)
    attended = oacc[...].T.astype(jnp.bfloat16)
    delta = attended.astype(jnp.float32) * g.astype(jnp.float32)
    delta = jnp.sum(delta.T, axis=0, keepdims=True)
    inverse = inverse * SCALE

    def grad_step(n, _):
        at = pl.multiple_of(low + n * STEP, BLOCK)
        k = kv[pl.ds(at, STEP), :HEAD]
        v = kv[pl.ds(at, STEP), HEAD:]
        dp = dot(v, g, NT)
        ds = (scores[n] * inverse * (dp - delta)).astype(jnp.bfloat16)
        qacc[...] += dot(k, ds, TN)
        acc[pl.ds(at, STEP), :HEAD] += dot(ds, q, NN)
        return 0

    lax.fori_loop(0, count, grad_step, 0)
    grad_q = qacc[...].T.astype(jnp.bfloat16)
    for h in range(GROUP):
        for half in range(2):
            rows = slice(h * BLOCK + half * 128, h * BLOCK + half * 128 + 128)
            out_ref[half, :, h * HEAD : (h + 1) * HEAD] = attended[rows]
            out_ref[half, :, (GROUP + h) * HEAD : (GROUP + h + 1) * HEAD] = grad_q[rows]

    @pl.when(tile == TILES - 1)
    def _():
        d2_ref[...] = acc[0:768].astype(jnp.bfloat16)
        d1_ref[...] = acc[768:1792].astype(jnp.bfloat16)
        d0_ref[...] = acc[1792:2816]


def attention(doc_lengths, qg, kv2, kv1, kv0):
    whole = lambda *shape: pl.BlockSpec(shape, lambda i: (0,) * len(shape))
    tiled = pl.BlockSpec((2, 128, 2 * GROUP * HEAD), lambda i: (i, 0, 0))
    return pl.pallas_call(
        attention_kernel,
        grid=(TILES,),
        in_specs=[
            pl.BlockSpec(memory_space=pltpu.SMEM),
            tiled,
            whole(768, 256),
            whole(1024, 256),
            whole(1024, 256),
        ],
        out_specs=[tiled, whole(768, 256), whole(1024, 256), whole(1024, 256)],
        out_shape=[
            jax.ShapeDtypeStruct((8, 128, 2 * GROUP * HEAD), jnp.bfloat16),
            jax.ShapeDtypeStruct((768, 256), jnp.bfloat16),
            jax.ShapeDtypeStruct((1024, 256), jnp.bfloat16),
            jax.ShapeDtypeStruct((1024, 256), jnp.float32),
        ],
        scratch_shapes=[
            pltpu.VMEM((WINDOW + STEP, 256), jnp.bfloat16),
            pltpu.VMEM((WINDOW + STEP, 256), jnp.float32),
            pltpu.VMEM((SLOTS, STEP, WIDE), jnp.float32),
            pltpu.VMEM((HEAD, WIDE), jnp.float32),
            pltpu.VMEM((HEAD, WIDE), jnp.float32),
        ],
        compiler_params=pltpu.CompilerParams(vmem_limit_bytes=48 * 1024 * 1024),
        name="attention",
    )(doc_lengths, qg, kv2, kv1, kv0)


def shift(x, by):
    pairs = [(i, i + by) for i in range(64) if 0 <= i + by < 64]
    return lax.ppermute(x, ("x", "y", "z"), pairs)


def swap(x):
    return lax.all_to_all(x, ROWS, split_axis=0, concat_axis=0, tiled=False)


def pack(a, b):
    tokens = a.shape[0]
    both = jnp.concatenate([a.reshape(tokens, 8, -1), b.reshape(tokens, 8, -1)], axis=2)
    return both.transpose(1, 0, 2)


def unpack(x):
    half = x.shape[2] // 2
    return [
        part.transpose(1, 0, 2).reshape(x.shape[1], 8 * half) for part in (x[:, :, :half], x[:, :, half:])
    ]


def body(doc_lengths, queries, keys, values, output_gradient):
    kv0 = swap(pack(keys, values)).reshape(ROW, 256)
    kv1 = shift(kv0, 4)
    kv2 = shift(kv0[256:], 8)
    qg = swap(pack(queries, output_gradient))
    out, d2, d1, d0 = attention(doc_lengths, qg, kv2, kv1, kv0)
    d1 = shift(d1, -4).astype(jnp.float32)
    d2 = shift(d2, -8).astype(jnp.float32)
    total = d0 + d1 + jnp.pad(d2, ((256, 0), (0, 0)))
    total, out = lax.optimization_barrier((total.astype(jnp.bfloat16), swap(out)))
    grad_keys, grad_values = unpack(swap(total.reshape(8, 128, 256)))
    attended, grad_queries = unpack(out)
    return attended, grad_queries, grad_keys, grad_values


def solution(mesh):
    grid = Mesh(mesh.devices.reshape(4, 4, 4, 2), AXES)
    tokens = P(AXES, None)
    return jax.shard_map(
        body,
        mesh=grid,
        in_specs=(P(None), tokens, tokens, tokens, tokens),
        out_specs=(tokens, tokens, tokens, tokens),
        check_vma=False,
    )
```

```python
import jax
import jax.numpy as jnp
from jax import lax
from jax.experimental import pallas as pl
from jax.experimental.pallas import tpu as pltpu
from jax.sharding import Mesh, PartitionSpec as P

HEAD = 128
GROUP = 4
BLOCK = 256
STEP = 1024
ROW = 1024
BEHIND = 1792
WINDOW = BEHIND + ROW
TILES = ROW // BLOCK
WIDE = GROUP * BLOCK
SCALE = HEAD ** (-0.5)
LOG2E = 1.4426950408889634
AXES = ("x", "y", "z", "hd")
ROWS = ("z", "hd")

NT = (((1,), (1,)), ((), ()))
TN = (((0,), (0,)), ((), ()))
NN = (((1,), (0,)), ((), ()))


def dot(a, b, dims):
    return lax.dot_general(a, b, dims, preferred_element_type=jnp.float32)


def attention_kernel(
    doc_ref, qg_ref, kv2_ref, kv1_ref, kv0_ref, out_ref, d2_ref, d1_ref, d0_ref, kv, acc, scores, oacc, qacc, top, sums
):
    tile = pl.program_id(0)
    row = lax.axis_index("x") * 4 + lax.axis_index("y")

    @pl.when(tile == 0)
    def _():
        kv[0:768] = kv2_ref[...]
        kv[768:1792] = kv1_ref[...]
        kv[1792:2816] = kv0_ref[...]
        acc[...] = jnp.zeros_like(acc)

    origin = row * ROW - BEHIND
    first_query = BEHIND + tile * BLOCK
    query_at = first_query + lax.broadcasted_iota(jnp.int32, (1, BLOCK), 1)
    start_at = jnp.full((1, BLOCK), -origin, jnp.int32)
    first_start = -origin
    end = -origin
    for n in range(16):
        end = end + doc_ref[n]
        start_at = jnp.where(query_at >= end, end, start_at)
        first_start = jnp.where(first_query >= end, end, first_start)
    low = first_start // BLOCK * BLOCK
    span = first_query + BLOCK - low
    steps = span // STEP
    rest = span - steps * STEP

    def sweep(step):
        def whole(n, _):
            step(pl.multiple_of(n * STEP, STEP), STEP)
            return 0

        lax.fori_loop(0, steps, whole, 0)
        for size in range(BLOCK, STEP, BLOCK):

            @pl.when(rest == size)
            def _():
                step(pl.multiple_of(steps * STEP, STEP), size)

    def keys_at(off, size):
        return pl.ds(pl.multiple_of(low + off, BLOCK), size)

    qg = qg_ref[...].reshape(BLOCK, 2 * GROUP * HEAD)
    q = jnp.concatenate([qg[:, h * HEAD : (h + 1) * HEAD] for h in range(GROUP)], axis=0)
    g = jnp.concatenate([qg[:, (GROUP + h) * HEAD : (GROUP + h + 1) * HEAD] for h in range(GROUP)], axis=0)

    top[...] = jnp.full_like(top, -jnp.inf)
    sums[...] = jnp.zeros_like(sums)
    oacc[...] = jnp.zeros_like(oacc)
    qacc[...] = jnp.zeros_like(qacc)

    def score_step(off, size):
        s = dot(kv[keys_at(off, size), :HEAD], q, NT)
        key_at = low + off + lax.broadcasted_iota(jnp.int32, (size, BLOCK), 0)
        allowed = (key_at >= start_at) & (key_at <= query_at)
        s = jnp.where(jnp.concatenate([allowed] * GROUP, axis=1), s, -jnp.inf)
        scores[pl.ds(off, size)] = s
        top[...] = jnp.maximum(top[...], jnp.max(s.reshape(size // 8, 8, WIDE), axis=0))

    sweep(score_step)
    peak = jnp.max(top[...], axis=0, keepdims=True)

    def exp_step(off, size):
        e = jnp.exp2((scores[pl.ds(off, size)] - peak) * (SCALE * LOG2E))
        scores[pl.ds(off, size)] = e
        sums[...] += jnp.sum(e.reshape(size // 8, 8, WIDE), axis=0)

    sweep(exp_step)
    inverse = 1.0 / jnp.sum(sums[...], axis=0, keepdims=True)

    def out_step(off, size):
        at = keys_at(off, size)
        p = (scores[pl.ds(off, size)] * inverse).astype(jnp.bfloat16)
        oacc[...] += dot(kv[at, HEAD:], p, TN)
        acc[at, HEAD:] += dot(p, g, NN)

    sweep(out_step)
    attended = oacc[...].astype(jnp.bfloat16)
    delta = jnp.sum(attended.astype(jnp.float32) * g.T.astype(jnp.float32), axis=0, keepdims=True)
    attended = attended.T
    inverse = inverse * SCALE

    def grad_step(off, size):
        at = keys_at(off, size)
        dp = dot(kv[at, HEAD:], g, NT)
        ds = (scores[pl.ds(off, size)] * inverse * (dp - delta)).astype(jnp.bfloat16)
        qacc[...] += dot(kv[at, :HEAD], ds, TN)
        acc[at, :HEAD] += dot(ds, q, NN)

    sweep(grad_step)
    grad_q = qacc[...].astype(jnp.bfloat16).T
    for h in range(GROUP):
        for half in range(BLOCK // 128):
            rows = slice(h * BLOCK + half * 128, h * BLOCK + half * 128 + 128)
            out_ref[half, :, h * HEAD : (h + 1) * HEAD] = attended[rows]
            out_ref[half, :, (GROUP + h) * HEAD : (GROUP + h + 1) * HEAD] = grad_q[rows]

    @pl.when(tile == TILES - 1)
    def _():
        d2_ref[...] = acc[0:768].astype(jnp.bfloat16)
        d1_ref[...] = acc[768:1792].astype(jnp.bfloat16)
        d0_ref[...] = acc[1792:2816]


def attention(doc_lengths, qg, kv2, kv1, kv0):
    whole = lambda *shape: pl.BlockSpec(shape, lambda i: (0,) * len(shape))
    tiled = pl.BlockSpec((2, 128, 2 * GROUP * HEAD), lambda i: (i, 0, 0))
    return pl.pallas_call(
        attention_kernel,
        grid=(TILES,),
        in_specs=[
            pl.BlockSpec(memory_space=pltpu.SMEM),
            tiled,
            whole(768, 256),
            whole(1024, 256),
            whole(1024, 256),
        ],
        out_specs=[tiled, whole(768, 256), whole(1024, 256), whole(1024, 256)],
        out_shape=[
            jax.ShapeDtypeStruct((8, 128, 2 * GROUP * HEAD), jnp.bfloat16),
            jax.ShapeDtypeStruct((768, 256), jnp.bfloat16),
            jax.ShapeDtypeStruct((1024, 256), jnp.bfloat16),
            jax.ShapeDtypeStruct((1024, 256), jnp.float32),
        ],
        scratch_shapes=[
            pltpu.VMEM((WINDOW, 256), jnp.bfloat16),
            pltpu.VMEM((WINDOW, 256), jnp.float32),
            pltpu.VMEM((BEHIND + BLOCK, WIDE), jnp.float32),
            pltpu.VMEM((HEAD, WIDE), jnp.float32),
            pltpu.VMEM((HEAD, WIDE), jnp.float32),
            pltpu.VMEM((8, WIDE), jnp.float32),
            pltpu.VMEM((8, WIDE), jnp.float32),
        ],
        compiler_params=pltpu.CompilerParams(vmem_limit_bytes=48 * 1024 * 1024),
        name="attention",
    )(doc_lengths, qg, kv2, kv1, kv0)


def shift(x, by):
    pairs = [(i, i + by) for i in range(64) if 0 <= i + by < 64]
    return lax.ppermute(x, ("x", "y", "z"), pairs)


def swap(x):
    return lax.all_to_all(x, ROWS, split_axis=0, concat_axis=0, tiled=False)


def pack_kernel(a_ref, b_ref, out_ref):
    groups, _, width = out_ref.shape
    for n in range(groups):
        columns = slice(n * (width // 2), (n + 1) * (width // 2))
        out_ref[n, :, : width // 2] = a_ref[:, columns]
        out_ref[n, :, width // 2 :] = b_ref[:, columns]


def pack(a, b, steps):
    tokens, width = a.shape
    return pl.pallas_call(
        pack_kernel,
        grid=(steps,),
        in_specs=[pl.BlockSpec((tokens, width // steps), lambda i: (0, i))] * 2,
        out_specs=pl.BlockSpec((8 // steps, tokens, width // 4), lambda i: (i, 0, 0)),
        out_shape=jax.ShapeDtypeStruct((8, tokens, width // 4), a.dtype),
        name="pack",
    )(a, b)


def unpack_kernel(x_ref, a_ref, b_ref):
    groups, _, width = x_ref.shape
    for n in range(groups):
        columns = slice(n * (width // 2), (n + 1) * (width // 2))
        a_ref[:, columns] = x_ref[n, :, : width // 2]
        b_ref[:, columns] = x_ref[n, :, width // 2 :]


def unpack(x, steps):
    _, tokens, half = x.shape
    width = half * 4
    return pl.pallas_call(
        unpack_kernel,
        grid=(steps,),
        in_specs=[pl.BlockSpec((8 // steps, tokens, half), lambda i: (i, 0, 0))],
        out_specs=[pl.BlockSpec((tokens, width // steps), lambda i: (0, i))] * 2,
        out_shape=[jax.ShapeDtypeStruct((tokens, width), x.dtype)] * 2,
        name="unpack",
    )(x)


def body(doc_lengths, queries, keys, values, output_gradient):
    kv0 = swap(pack(keys, values, 1)).reshape(ROW, 256)
    kv1 = shift(kv0, 4)
    kv2 = shift(kv0[256:], 8)
    qg = swap(pack(queries, output_gradient, 4))
    out, d2, d1, d0 = attention(doc_lengths, qg, kv2, kv1, kv0)
    d1 = shift(d1, -4).astype(jnp.float32)
    d2 = shift(d2, -8).astype(jnp.float32)
    total = d0 + d1 + jnp.pad(d2, ((256, 0), (0, 0)))
    total, out = lax.optimization_barrier((total.astype(jnp.bfloat16), swap(out)))
    grad_keys, grad_values = unpack(swap(total.reshape(8, 128, 256)), 1)
    attended, grad_queries = unpack(out, 4)
    return attended, grad_queries, grad_keys, grad_values


def solution(mesh):
    grid = Mesh(mesh.devices.reshape(4, 4, 4, 2), AXES)
    tokens = P(AXES, None)
    return jax.shard_map(
        body,
        mesh=grid,
        in_specs=(P(None), tokens, tokens, tokens, tokens),
        out_specs=(tokens, tokens, tokens, tokens),
        check_vma=False,
    )
```

```python
import jax
import jax.numpy as jnp
from jax import lax
from jax.experimental import pallas as pl
from jax.experimental.pallas import tpu as pltpu
from jax.sharding import Mesh, PartitionSpec as P

HEAD = 128
GROUP = 4
BLOCK = 256
STEP = 1024
ROW = 1024
BEHIND = 1792
WINDOW = BEHIND + ROW
TILES = ROW // BLOCK
WIDE = GROUP * BLOCK
SCALE = HEAD ** (-0.5)
LOG2E = 1.4426950408889634
AXES = ("x", "y", "z", "hd")
ROWS = ("z", "hd")

NT = (((1,), (1,)), ((), ()))
TN = (((0,), (0,)), ((), ()))
NN = (((1,), (0,)), ((), ()))


def dot(a, b, dims):
    return lax.dot_general(a, b, dims, preferred_element_type=jnp.float32)


def attention_kernel(
    doc_ref, qg_ref, kv2_ref, kv1_ref, kv0_ref, out_ref, d2_ref, d1_ref, d0_ref, kv, acc, scores, oacc, qacc, top, sums
):
    tile = pl.program_id(0)
    row = lax.axis_index("x") * 4 + lax.axis_index("y")

    @pl.when(tile == 0)
    def _():
        kv[0:768] = kv2_ref[...]
        kv[768:1792] = kv1_ref[...]
        kv[1792:2816] = kv0_ref[...]
        acc[...] = jnp.zeros_like(acc)

    origin = row * ROW - BEHIND
    first_query = BEHIND + tile * BLOCK
    query_at = first_query + lax.broadcasted_iota(jnp.int32, (1, BLOCK), 1)
    start_at = jnp.full((1, BLOCK), -origin, jnp.int32)
    first_start = -origin
    end = -origin
    for n in range(16):
        end = end + doc_ref[n]
        start_at = jnp.where(query_at >= end, end, start_at)
        first_start = jnp.where(first_query >= end, end, first_start)
    low = first_start // BLOCK * BLOCK
    span = first_query + BLOCK - low
    steps = span // STEP
    rest = span - steps * STEP

    def sweep(step):
        def whole(n, _):
            step(pl.multiple_of(n * STEP, STEP), STEP)
            return 0

        lax.fori_loop(0, steps, whole, 0)
        for size in range(BLOCK, STEP, BLOCK):

            @pl.when(rest == size)
            def _():
                step(pl.multiple_of(steps * STEP, STEP), size)

    def keys_at(off, size):
        return pl.ds(pl.multiple_of(low + off, BLOCK), size)

    qg = qg_ref[...].reshape(BLOCK, 2 * GROUP * HEAD)
    q = jnp.concatenate([qg[:, h * HEAD : (h + 1) * HEAD] for h in range(GROUP)], axis=0)
    g = jnp.concatenate([qg[:, (GROUP + h) * HEAD : (GROUP + h + 1) * HEAD] for h in range(GROUP)], axis=0)

    top[...] = jnp.full_like(top, -jnp.inf)
    sums[...] = jnp.zeros_like(sums)
    oacc[...] = jnp.zeros_like(oacc)
    qacc[...] = jnp.zeros_like(qacc)

    def score_step(off, size):
        s = dot(kv[keys_at(off, size), :HEAD], q, NT)
        key_at = low + off + lax.broadcasted_iota(jnp.int32, (size, BLOCK), 0)
        allowed = (key_at >= start_at) & (key_at <= query_at)
        s = jnp.where(jnp.concatenate([allowed] * GROUP, axis=1), s, -jnp.inf)
        scores[pl.ds(off, size)] = s
        top[...] = jnp.maximum(top[...], jnp.max(s.reshape(size // 8, 8, WIDE), axis=0))

    sweep(score_step)
    peak = jnp.max(top[...], axis=0, keepdims=True)

    def exp_step(off, size):
        e = jnp.exp2((scores[pl.ds(off, size)] - peak) * (SCALE * LOG2E))
        scores[pl.ds(off, size)] = e
        sums[...] += jnp.sum(e.reshape(size // 8, 8, WIDE), axis=0)

    sweep(exp_step)
    inverse = 1.0 / jnp.sum(sums[...], axis=0, keepdims=True)

    def out_step(off, size):
        at = keys_at(off, size)
        p = (scores[pl.ds(off, size)] * inverse).astype(jnp.bfloat16)
        oacc[...] += dot(kv[at, HEAD:], p, TN)
        acc[at, HEAD:] += dot(p, g, NN)

    sweep(out_step)
    attended = oacc[...].astype(jnp.bfloat16)
    delta = jnp.sum(attended.astype(jnp.float32) * g.T.astype(jnp.float32), axis=0, keepdims=True)
    attended = attended.T
    inverse = inverse * SCALE

    def grad_step(off, size):
        at = keys_at(off, size)
        dp = dot(kv[at, HEAD:], g, NT)
        ds = (scores[pl.ds(off, size)] * inverse * (dp - delta)).astype(jnp.bfloat16)
        qacc[...] += dot(kv[at, :HEAD], ds, TN)
        acc[at, :HEAD] += dot(ds, q, NN)

    sweep(grad_step)
    grad_q = qacc[...].astype(jnp.bfloat16).T
    for h in range(GROUP):
        for half in range(BLOCK // 128):
            rows = slice(h * BLOCK + half * 128, h * BLOCK + half * 128 + 128)
            out_ref[half, :, h * HEAD : (h + 1) * HEAD] = attended[rows]
            out_ref[half, :, (GROUP + h) * HEAD : (GROUP + h + 1) * HEAD] = grad_q[rows]

    @pl.when(tile == TILES - 1)
    def _():
        d2_ref[...] = acc[0:768].astype(jnp.bfloat16)
        d1_ref[...] = acc[768:1792].astype(jnp.bfloat16)
        d0_ref[...] = acc[1792:2816]


def attention(doc_lengths, qg, kv2, kv1, kv0):
    whole = lambda *shape: pl.BlockSpec(shape, lambda i: (0,) * len(shape))
    tiled = pl.BlockSpec((2, 128, 2 * GROUP * HEAD), lambda i: (i, 0, 0))
    return pl.pallas_call(
        attention_kernel,
        grid=(TILES,),
        in_specs=[
            pl.BlockSpec(memory_space=pltpu.SMEM),
            tiled,
            whole(768, 256),
            whole(1024, 256),
            whole(1024, 256),
        ],
        out_specs=[tiled, whole(768, 256), whole(1024, 256), whole(1024, 256)],
        out_shape=[
            jax.ShapeDtypeStruct((8, 128, 2 * GROUP * HEAD), jnp.bfloat16),
            jax.ShapeDtypeStruct((768, 256), jnp.bfloat16),
            jax.ShapeDtypeStruct((1024, 256), jnp.bfloat16),
            jax.ShapeDtypeStruct((1024, 256), jnp.float32),
        ],
        scratch_shapes=[
            pltpu.VMEM((WINDOW, 256), jnp.bfloat16),
            pltpu.VMEM((WINDOW, 256), jnp.float32),
            pltpu.VMEM((BEHIND + BLOCK, WIDE), jnp.float32),
            pltpu.VMEM((HEAD, WIDE), jnp.float32),
            pltpu.VMEM((HEAD, WIDE), jnp.float32),
            pltpu.VMEM((8, WIDE), jnp.float32),
            pltpu.VMEM((8, WIDE), jnp.float32),
        ],
        compiler_params=pltpu.CompilerParams(vmem_limit_bytes=48 * 1024 * 1024),
        name="attention",
    )(doc_lengths, qg, kv2, kv1, kv0)


def shift(x, by):
    pairs = [(i, i + by) for i in range(64) if 0 <= i + by < 64]
    return lax.ppermute(x, ("x", "y", "z"), pairs)


def swap(x):
    return lax.all_to_all(x, ROWS, split_axis=0, concat_axis=0, tiled=False)


def pack_kernel(a_ref, b_ref, out_ref):
    groups, _, width = out_ref.shape
    for n in range(groups):
        columns = slice(n * (width // 2), (n + 1) * (width // 2))
        out_ref[n, :, : width // 2] = a_ref[:, columns]
        out_ref[n, :, width // 2 :] = b_ref[:, columns]


def pack(a, b, steps):
    tokens, width = a.shape
    return pl.pallas_call(
        pack_kernel,
        grid=(steps,),
        in_specs=[pl.BlockSpec((tokens, width // steps), lambda i: (0, i))] * 2,
        out_specs=pl.BlockSpec((8 // steps, tokens, width // 4), lambda i: (i, 0, 0)),
        out_shape=jax.ShapeDtypeStruct((8, tokens, width // 4), a.dtype),
        name="pack",
    )(a, b)


def unpack_kernel(x_ref, a_ref, b_ref):
    groups, _, width = x_ref.shape
    for n in range(groups):
        columns = slice(n * (width // 2), (n + 1) * (width // 2))
        a_ref[:, columns] = x_ref[n, :, : width // 2]
        b_ref[:, columns] = x_ref[n, :, width // 2 :]


def unpack(x, steps, limit=None):
    _, tokens, half = x.shape
    width = half * 4
    return pl.pallas_call(
        unpack_kernel,
        grid=(steps,),
        in_specs=[pl.BlockSpec((8 // steps, tokens, half), lambda i: (i, 0, 0))],
        out_specs=[pl.BlockSpec((tokens, width // steps), lambda i: (0, i))] * 2,
        out_shape=[jax.ShapeDtypeStruct((tokens, width), x.dtype)] * 2,
        compiler_params=pltpu.CompilerParams(vmem_limit_bytes=limit),
        name="unpack",
    )(x)


def body(doc_lengths, queries, keys, values, output_gradient):
    kv0 = swap(pack(keys, values, 1)).reshape(ROW, 256)
    kv1 = shift(kv0, 4)
    kv2 = shift(kv0[256:], 8)
    qg = swap(pack(queries, output_gradient, 4))
    out, d2, d1, d0 = attention(doc_lengths, qg, kv2, kv1, kv0)
    d1 = shift(d1, -4).astype(jnp.float32)
    d2 = shift(d2, -8).astype(jnp.float32)
    total = d0 + d1 + jnp.pad(d2, ((256, 0), (0, 0)))
    total, out = lax.optimization_barrier((total.astype(jnp.bfloat16), swap(out)))
    grad_keys, grad_values = unpack(swap(total.reshape(8, 128, 256)), 1, 8 * 1024 * 1024)
    attended, grad_queries = unpack(out, 4)
    return attended, grad_queries, grad_keys, grad_values


def solution(mesh):
    grid = Mesh(mesh.devices.reshape(4, 4, 4, 2), AXES)
    tokens = P(AXES, None)
    return jax.shard_map(
        body,
        mesh=grid,
        in_specs=(P(None), tokens, tokens, tokens, tokens),
        out_specs=(tokens, tokens, tokens, tokens),
        check_vma=False,
    )
```

```python
import jax
import jax.numpy as jnp
from jax import lax
from jax.experimental import pallas as pl
from jax.experimental.pallas import tpu as pltpu
from jax.sharding import Mesh, PartitionSpec as P

HEAD = 128
GROUP = 4
BLOCK = 256
STEP = 1024
ROW = 1024
BEHIND = 1792
WINDOW = BEHIND + ROW
TILES = ROW // BLOCK
WIDE = GROUP * BLOCK
SCALE = HEAD ** (-0.5)
LOG2E = 1.4426950408889634
AXES = ("x", "y", "z", "hd")
ROWS = ("z", "hd")

NT = (((1,), (1,)), ((), ()))
TN = (((0,), (0,)), ((), ()))
NN = (((1,), (0,)), ((), ()))


def dot(a, b, dims):
    return lax.dot_general(a, b, dims, preferred_element_type=jnp.float32)


def attention_kernel(
    doc_ref, qg_ref, kv2_ref, kv1_ref, kv0_ref, out_ref, d2_ref, d1_ref, d0_ref, kv, acc, scores, oacc, qacc, top, sums
):
    tile = pl.program_id(0)
    row = lax.axis_index("x") * 4 + lax.axis_index("y")

    @pl.when(tile == 0)
    def _():
        kv[0:768] = kv2_ref[...]
        kv[768:1792] = kv1_ref[...]
        kv[1792:2816] = kv0_ref[...]
        acc[...] = jnp.zeros_like(acc)

    origin = row * ROW - BEHIND
    first_query = BEHIND + tile * BLOCK
    query_at = first_query + lax.broadcasted_iota(jnp.int32, (1, BLOCK), 1)
    start_at = jnp.full((1, BLOCK), -origin, jnp.int32)
    first_start = -origin
    end = -origin
    for n in range(16):
        end = end + doc_ref[n]
        start_at = jnp.where(query_at >= end, end, start_at)
        first_start = jnp.where(first_query >= end, end, first_start)
    low = first_start // BLOCK * BLOCK
    span = first_query + BLOCK - low
    steps = span // STEP
    rest = span - steps * STEP

    def sweep(step):
        def whole(n, _):
            step(pl.multiple_of(n * STEP, STEP), STEP)
            return 0

        lax.fori_loop(0, steps, whole, 0)
        for size in range(BLOCK, STEP, BLOCK):

            @pl.when(rest == size)
            def _():
                step(pl.multiple_of(steps * STEP, STEP), size)

    def keys_at(off, size):
        return pl.ds(pl.multiple_of(low + off, BLOCK), size)

    qg = qg_ref[...].reshape(BLOCK, 2 * GROUP * HEAD)
    q = jnp.concatenate([qg[:, h * HEAD : (h + 1) * HEAD] for h in range(GROUP)], axis=0)
    g = jnp.concatenate([qg[:, (GROUP + h) * HEAD : (GROUP + h + 1) * HEAD] for h in range(GROUP)], axis=0)

    top[...] = jnp.full_like(top, -jnp.inf)
    sums[...] = jnp.zeros_like(sums)
    oacc[...] = jnp.zeros_like(oacc)
    qacc[...] = jnp.zeros_like(qacc)

    def score_step(off, size):
        s = dot(kv[keys_at(off, size), :HEAD], q, NT)
        key_at = low + off + lax.broadcasted_iota(jnp.int32, (size, BLOCK), 0)
        allowed = (key_at >= start_at) & (key_at <= query_at)
        s = jnp.where(jnp.concatenate([allowed] * GROUP, axis=1), s, -jnp.inf)
        scores[pl.ds(off, size)] = s
        top[...] = jnp.maximum(top[...], jnp.max(s.reshape(size // 8, 8, WIDE), axis=0))

    sweep(score_step)
    peak = jnp.max(top[...], axis=0, keepdims=True)

    def exp_step(off, size):
        e = jnp.exp2((scores[pl.ds(off, size)] - peak) * (SCALE * LOG2E))
        scores[pl.ds(off, size)] = e
        sums[...] += jnp.sum(e.reshape(size // 8, 8, WIDE), axis=0)

    sweep(exp_step)
    inverse = 1.0 / jnp.sum(sums[...], axis=0, keepdims=True)

    def out_step(off, size):
        at = keys_at(off, size)
        p = (scores[pl.ds(off, size)] * inverse).astype(jnp.bfloat16)
        oacc[...] += dot(kv[at, HEAD:], p, TN)
        acc[at, HEAD:] += dot(p, g, NN)

    sweep(out_step)
    attended = oacc[...].astype(jnp.bfloat16)
    delta = jnp.sum(attended.astype(jnp.float32) * g.T.astype(jnp.float32), axis=0, keepdims=True)
    attended = attended.T
    inverse = inverse * SCALE

    def grad_step(off, size):
        at = keys_at(off, size)
        dp = dot(kv[at, HEAD:], g, NT)
        ds = (scores[pl.ds(off, size)] * inverse * (dp - delta)).astype(jnp.bfloat16)
        qacc[...] += dot(kv[at, :HEAD], ds, TN)
        acc[at, :HEAD] += dot(ds, q, NN)

    sweep(grad_step)
    grad_q = qacc[...].astype(jnp.bfloat16).T
    for h in range(GROUP):
        for half in range(BLOCK // 128):
            rows = slice(h * BLOCK + half * 128, h * BLOCK + half * 128 + 128)
            out_ref[half, :, h * HEAD : (h + 1) * HEAD] = attended[rows]
            out_ref[half, :, (GROUP + h) * HEAD : (GROUP + h + 1) * HEAD] = grad_q[rows]

    @pl.when(tile == TILES - 1)
    def _():
        d2_ref[...] = acc[0:768].astype(jnp.bfloat16)
        d1_ref[...] = acc[768:1792].astype(jnp.bfloat16)
        d0_ref[...] = acc[1792:2816]


def attention(doc_lengths, qg, kv2, kv1, kv0):
    whole = lambda *shape: pl.BlockSpec(shape, lambda i: (0,) * len(shape))
    tiled = pl.BlockSpec((2, 128, 2 * GROUP * HEAD), lambda i: (i, 0, 0))
    return pl.pallas_call(
        attention_kernel,
        grid=(TILES,),
        in_specs=[
            pl.BlockSpec(memory_space=pltpu.SMEM),
            tiled,
            whole(768, 256),
            whole(1024, 256),
            whole(1024, 256),
        ],
        out_specs=[tiled, whole(768, 256), whole(1024, 256), whole(1024, 256)],
        out_shape=[
            jax.ShapeDtypeStruct((8, 128, 2 * GROUP * HEAD), jnp.bfloat16),
            jax.ShapeDtypeStruct((768, 256), jnp.bfloat16),
            jax.ShapeDtypeStruct((1024, 256), jnp.bfloat16),
            jax.ShapeDtypeStruct((1024, 256), jnp.float32),
        ],
        scratch_shapes=[
            pltpu.VMEM((WINDOW, 256), jnp.bfloat16),
            pltpu.VMEM((WINDOW, 256), jnp.float32),
            pltpu.VMEM((BEHIND + BLOCK, WIDE), jnp.float32),
            pltpu.VMEM((HEAD, WIDE), jnp.float32),
            pltpu.VMEM((HEAD, WIDE), jnp.float32),
            pltpu.VMEM((8, WIDE), jnp.float32),
            pltpu.VMEM((8, WIDE), jnp.float32),
        ],
        compiler_params=pltpu.CompilerParams(vmem_limit_bytes=48 * 1024 * 1024),
        name="attention",
    )(doc_lengths, qg, kv2, kv1, kv0)


def shift(x, by):
    pairs = [(i, i + by) for i in range(64) if 0 <= i + by < 64]
    return lax.ppermute(x, ("x", "y", "z"), pairs)


def between(i):
    return i + 4 if i // 4 % 4 == 2 else i - 12


def shift_two(x, back):
    first = [(i, between(i)) for i in range(8, 64)]
    second = [(between(i), i - 8) for i in range(8, 64)]
    if not back:
        first, second = [(b, a) for a, b in second], [(b, a) for a, b in first]
    for pairs in (first, second):
        x = lax.ppermute(x, ("x", "y", "z"), pairs)
    return x


def swap(x):
    return lax.all_to_all(x, ROWS, split_axis=0, concat_axis=0, tiled=False)


def pack_kernel(a_ref, b_ref, out_ref):
    groups, _, width = out_ref.shape
    for n in range(groups):
        columns = slice(n * (width // 2), (n + 1) * (width // 2))
        out_ref[n, :, : width // 2] = a_ref[:, columns]
        out_ref[n, :, width // 2 :] = b_ref[:, columns]


def pack(a, b, steps):
    tokens, width = a.shape
    return pl.pallas_call(
        pack_kernel,
        grid=(steps,),
        in_specs=[pl.BlockSpec((tokens, width // steps), lambda i: (0, i))] * 2,
        out_specs=pl.BlockSpec((8 // steps, tokens, width // 4), lambda i: (i, 0, 0)),
        out_shape=jax.ShapeDtypeStruct((8, tokens, width // 4), a.dtype),
        name="pack",
    )(a, b)


def unpack_kernel(x_ref, a_ref, b_ref):
    groups, _, width = x_ref.shape
    for n in range(groups):
        columns = slice(n * (width // 2), (n + 1) * (width // 2))
        a_ref[:, columns] = x_ref[n, :, : width // 2]
        b_ref[:, columns] = x_ref[n, :, width // 2 :]


def unpack(x, steps, limit=None):
    _, tokens, half = x.shape
    width = half * 4
    return pl.pallas_call(
        unpack_kernel,
        grid=(steps,),
        in_specs=[pl.BlockSpec((8 // steps, tokens, half), lambda i: (i, 0, 0))],
        out_specs=[pl.BlockSpec((tokens, width // steps), lambda i: (0, i))] * 2,
        out_shape=[jax.ShapeDtypeStruct((tokens, width), x.dtype)] * 2,
        compiler_params=pltpu.CompilerParams(vmem_limit_bytes=limit),
        name="unpack",
    )(x)


def body(doc_lengths, queries, keys, values, output_gradient):
    kv0 = swap(pack(keys, values, 1)).reshape(ROW, 256)
    kv1 = shift(kv0, 4)
    kv2 = shift_two(kv0[256:], False)
    qg = swap(pack(queries, output_gradient, 4))
    out, d2, d1, d0 = attention(doc_lengths, qg, kv2, kv1, kv0)
    d1 = shift(d1, -4).astype(jnp.float32)
    d2 = shift_two(d2, True).astype(jnp.float32)
    total = d0 + d1 + jnp.pad(d2, ((256, 0), (0, 0)))
    total, out = lax.optimization_barrier((total.astype(jnp.bfloat16), swap(out)))
    grad_keys, grad_values = unpack(swap(total.reshape(8, 128, 256)), 1, 8 * 1024 * 1024)
    attended, grad_queries = unpack(out, 4)
    return attended, grad_queries, grad_keys, grad_values


def solution(mesh):
    grid = Mesh(mesh.devices.reshape(4, 4, 4, 2), AXES)
    tokens = P(AXES, None)
    return jax.shard_map(
        body,
        mesh=grid,
        in_specs=(P(None), tokens, tokens, tokens, tokens),
        out_specs=(tokens, tokens, tokens, tokens),
        check_vma=False,
    )
```

```python
import jax
import jax.numpy as jnp
from jax import lax
from jax.experimental import pallas as pl
from jax.experimental.pallas import tpu as pltpu
from jax.sharding import Mesh, PartitionSpec as P

HEAD = 128
GROUP = 4
BLOCK = 256
STEP = 1536
ROW = 1024
BEHIND = 1792
WINDOW = BEHIND + ROW
TILES = ROW // BLOCK
WIDE = GROUP * BLOCK
SCALE = HEAD ** (-0.5)
LOG2E = 1.4426950408889634
AXES = ("x", "y", "z", "hd")
ROWS = ("z", "hd")

NT = (((1,), (1,)), ((), ()))
TN = (((0,), (0,)), ((), ()))
NN = (((1,), (0,)), ((), ()))


def dot(a, b, dims):
    return lax.dot_general(a, b, dims, preferred_element_type=jnp.float32)


def attention_kernel(
    doc_ref, qg_ref, kv2_ref, kv1_ref, kv0_ref, out_ref, d2_ref, d1_ref, d0_ref, kv, acc, scores, oacc, qacc, top, sums
):
    tile = pl.program_id(0)
    row = lax.axis_index("x") * 4 + lax.axis_index("y")

    @pl.when(tile == 0)
    def _():
        kv[0:768] = kv2_ref[...]
        kv[768:1792] = kv1_ref[...]
        kv[1792:2816] = kv0_ref[...]
        acc[...] = jnp.zeros_like(acc)

    origin = row * ROW - BEHIND
    first_query = BEHIND + tile * BLOCK
    query_at = first_query + lax.broadcasted_iota(jnp.int32, (1, BLOCK), 1)
    start_at = jnp.full((1, BLOCK), -origin, jnp.int32)
    first_start = -origin
    end = -origin
    for n in range(16):
        end = end + doc_ref[n]
        start_at = jnp.where(query_at >= end, end, start_at)
        first_start = jnp.where(first_query >= end, end, first_start)
    low = first_start // BLOCK * BLOCK
    span = first_query + BLOCK - low
    steps = span // STEP
    rest = span - steps * STEP

    def sweep(step):
        def whole(n, _):
            step(pl.multiple_of(n * STEP, STEP), STEP)
            return 0

        lax.fori_loop(0, steps, whole, 0)
        for size in range(BLOCK, STEP, BLOCK):

            @pl.when(rest == size)
            def _():
                step(pl.multiple_of(steps * STEP, STEP), size)

    def keys_at(off, size):
        return pl.ds(pl.multiple_of(low + off, BLOCK), size)

    qg = qg_ref[...].reshape(BLOCK, 2 * GROUP * HEAD)
    q = jnp.concatenate([qg[:, h * HEAD : (h + 1) * HEAD] for h in range(GROUP)], axis=0)
    g = jnp.concatenate([qg[:, (GROUP + h) * HEAD : (GROUP + h + 1) * HEAD] for h in range(GROUP)], axis=0)

    top[...] = jnp.full_like(top, -jnp.inf)
    sums[...] = jnp.zeros_like(sums)
    oacc[...] = jnp.zeros_like(oacc)
    qacc[...] = jnp.zeros_like(qacc)

    def score_step(off, size):
        s = dot(kv[keys_at(off, size), :HEAD], q, NT)
        key_at = low + off + lax.broadcasted_iota(jnp.int32, (size, BLOCK), 0)
        allowed = (key_at >= start_at) & (key_at <= query_at)
        s = jnp.where(jnp.concatenate([allowed] * GROUP, axis=1), s, -jnp.inf)
        scores[pl.ds(off, size)] = s
        top[...] = jnp.maximum(top[...], jnp.max(s.reshape(size // 8, 8, WIDE), axis=0))

    sweep(score_step)
    peak = jnp.max(top[...], axis=0, keepdims=True)

    def exp_step(off, size):
        e = jnp.exp2((scores[pl.ds(off, size)] - peak) * (SCALE * LOG2E))
        scores[pl.ds(off, size)] = e
        sums[...] += jnp.sum(e.reshape(size // 8, 8, WIDE), axis=0)

    sweep(exp_step)
    inverse = 1.0 / jnp.sum(sums[...], axis=0, keepdims=True)

    def out_step(off, size):
        at = keys_at(off, size)
        p = (scores[pl.ds(off, size)] * inverse).astype(jnp.bfloat16)
        oacc[...] += dot(kv[at, HEAD:], p, TN)
        acc[at, HEAD:] += dot(p, g, NN)

    sweep(out_step)
    attended = oacc[...].astype(jnp.bfloat16)
    delta = jnp.sum(attended.astype(jnp.float32) * g.T.astype(jnp.float32), axis=0, keepdims=True)
    attended = attended.T
    inverse = inverse * SCALE

    def grad_step(off, size):
        at = keys_at(off, size)
        dp = dot(kv[at, HEAD:], g, NT)
        ds = (scores[pl.ds(off, size)] * inverse * (dp - delta)).astype(jnp.bfloat16)
        qacc[...] += dot(kv[at, :HEAD], ds, TN)
        acc[at, :HEAD] += dot(ds, q, NN)

    sweep(grad_step)
    grad_q = qacc[...].astype(jnp.bfloat16).T
    for h in range(GROUP):
        for half in range(BLOCK // 128):
            rows = slice(h * BLOCK + half * 128, h * BLOCK + half * 128 + 128)
            out_ref[half, :, h * HEAD : (h + 1) * HEAD] = attended[rows]
            out_ref[half, :, (GROUP + h) * HEAD : (GROUP + h + 1) * HEAD] = grad_q[rows]

    @pl.when(tile == TILES - 1)
    def _():
        d2_ref[...] = acc[0:768].astype(jnp.bfloat16)
        d1_ref[...] = acc[768:1792].astype(jnp.bfloat16)
        d0_ref[...] = acc[1792:2816]


def attention(doc_lengths, qg, kv2, kv1, kv0):
    whole = lambda *shape: pl.BlockSpec(shape, lambda i: (0,) * len(shape))
    tiled = pl.BlockSpec((2, 128, 2 * GROUP * HEAD), lambda i: (i, 0, 0))
    return pl.pallas_call(
        attention_kernel,
        grid=(TILES,),
        in_specs=[
            pl.BlockSpec(memory_space=pltpu.SMEM),
            tiled,
            whole(768, 256),
            whole(1024, 256),
            whole(1024, 256),
        ],
        out_specs=[tiled, whole(768, 256), whole(1024, 256), whole(1024, 256)],
        out_shape=[
            jax.ShapeDtypeStruct((8, 128, 2 * GROUP * HEAD), jnp.bfloat16),
            jax.ShapeDtypeStruct((768, 256), jnp.bfloat16),
            jax.ShapeDtypeStruct((1024, 256), jnp.bfloat16),
            jax.ShapeDtypeStruct((1024, 256), jnp.float32),
        ],
        scratch_shapes=[
            pltpu.VMEM((WINDOW, 256), jnp.bfloat16),
            pltpu.VMEM((WINDOW, 256), jnp.float32),
            pltpu.VMEM((BEHIND + BLOCK, WIDE), jnp.float32),
            pltpu.VMEM((HEAD, WIDE), jnp.float32),
            pltpu.VMEM((HEAD, WIDE), jnp.float32),
            pltpu.VMEM((8, WIDE), jnp.float32),
            pltpu.VMEM((8, WIDE), jnp.float32),
        ],
        compiler_params=pltpu.CompilerParams(vmem_limit_bytes=48 * 1024 * 1024),
        name="attention",
    )(doc_lengths, qg, kv2, kv1, kv0)


def shift(x, by):
    pairs = [(i, i + by) for i in range(64) if 0 <= i + by < 64]
    return lax.ppermute(x, ("x", "y", "z"), pairs)


def between(i):
    return i + 4 if i // 4 % 4 == 2 else i - 12


def shift_two(x, back):
    first = [(i, between(i)) for i in range(8, 64)]
    second = [(between(i), i - 8) for i in range(8, 64)]
    if not back:
        first, second = [(b, a) for a, b in second], [(b, a) for a, b in first]
    for pairs in (first, second):
        x = lax.ppermute(x, ("x", "y", "z"), pairs)
    return x


def swap(x):
    return lax.all_to_all(x, ROWS, split_axis=0, concat_axis=0, tiled=False)


def pack_kernel(a_ref, b_ref, out_ref):
    groups, _, width = out_ref.shape
    for n in range(groups):
        columns = slice(n * (width // 2), (n + 1) * (width // 2))
        out_ref[n, :, : width // 2] = a_ref[:, columns]
        out_ref[n, :, width // 2 :] = b_ref[:, columns]


def pack(a, b, steps):
    tokens, width = a.shape
    return pl.pallas_call(
        pack_kernel,
        grid=(steps,),
        in_specs=[pl.BlockSpec((tokens, width // steps), lambda i: (0, i))] * 2,
        out_specs=pl.BlockSpec((8 // steps, tokens, width // 4), lambda i: (i, 0, 0)),
        out_shape=jax.ShapeDtypeStruct((8, tokens, width // 4), a.dtype),
        name="pack",
    )(a, b)


def unpack_kernel(x_ref, a_ref, b_ref):
    groups, _, width = x_ref.shape
    for n in range(groups):
        columns = slice(n * (width // 2), (n + 1) * (width // 2))
        a_ref[:, columns] = x_ref[n, :, : width // 2]
        b_ref[:, columns] = x_ref[n, :, width // 2 :]


def unpack(x, steps, limit=None):
    _, tokens, half = x.shape
    width = half * 4
    return pl.pallas_call(
        unpack_kernel,
        grid=(steps,),
        in_specs=[pl.BlockSpec((8 // steps, tokens, half), lambda i: (i, 0, 0))],
        out_specs=[pl.BlockSpec((tokens, width // steps), lambda i: (0, i))] * 2,
        out_shape=[jax.ShapeDtypeStruct((tokens, width), x.dtype)] * 2,
        compiler_params=pltpu.CompilerParams(vmem_limit_bytes=limit),
        name="unpack",
    )(x)


def body(doc_lengths, queries, keys, values, output_gradient):
    kv0 = swap(pack(keys, values, 1)).reshape(ROW, 256)
    kv1 = shift(kv0, 4)
    kv2 = shift_two(kv0[256:], False)
    qg = swap(pack(queries, output_gradient, 4))
    out, d2, d1, d0 = attention(doc_lengths, qg, kv2, kv1, kv0)
    d1 = shift(d1, -4).astype(jnp.float32)
    d2 = shift_two(d2, True).astype(jnp.float32)
    total = d0 + d1 + jnp.pad(d2, ((256, 0), (0, 0)))
    total, out = lax.optimization_barrier((total.astype(jnp.bfloat16), swap(out)))
    grad_keys, grad_values = unpack(swap(total.reshape(8, 128, 256)), 1, 8 * 1024 * 1024)
    attended, grad_queries = unpack(out, 4)
    return attended, grad_queries, grad_keys, grad_values


def solution(mesh):
    grid = Mesh(mesh.devices.reshape(4, 4, 4, 2), AXES)
    tokens = P(AXES, None)
    return jax.shard_map(
        body,
        mesh=grid,
        in_specs=(P(None), tokens, tokens, tokens, tokens),
        out_specs=(tokens, tokens, tokens, tokens),
        check_vma=False,
    )
```
